32 devices in a mesh: dp: 4 (over y, x), tm: 8 (over z, core).
Axes of the slice: x: 2, y: 2, z: 4, core: 2. Of those that a mesh axis runs over, the one named last changes fastest.
Arguments:
- activations: bfloat16 [4, 16, 64, 16, 128], P('dp', 'tm')
- conv_weight: bfloat16 [3, 3, 3, 128, 128], replicated, may hold values from -0.109375 to 0.109375
- norm_gain: float32 [128], replicated, may hold values from 0.5 to 1.5
- norm_bias: float32 [128], replicated, may hold values from -0.5 to 0.5
- down_weight: bfloat16 [3, 3, 128, 128], replicated, may hold values from -0.1875 to 0.1875
- cotangent: bfloat16 [4, 16, 32, 8, 128], P('dp', None, 'tm'), may hold values from -0.625 to 0.625
Outputs:
- encoded: bfloat16 [4, 16, 32, 8, 128], P('dp', None, 'tm')
- grad_down: float32 [3, 3, 128, 128], P(None, None, None, 'tm')
The draws below stay inside these ranges and needn't reach their ends.
All inputs are finite; a program needn't handle non-finite values.
Results may differ from the reference program's by a relative error of at most 0.005.
Values may be sent and summed in bfloat16 or wider, within the bound.
No kernel may reach another device: no remote copies, remote signals or barrier semaphores. Data moves between devices by JAX's collectives and lax.ppermute only.
A program may use at most 64 MiB of HBM per device.

```python
import math
import jax
import jax.numpy as jnp
from jax import lax

C = 128
C2 = 128
G = 32
H = 64
W = 16
CLIPS = 4
FRAMES = 16
H2 = 32
W2 = 8


def draw_activations(key, part):
    key_base = jax.random.fold_in(key, 0)
    key_chan = jax.random.fold_in(key, 1)
    key_frames = jax.random.fold_in(key, 3)
    key_flip = jax.random.fold_in(key, 4)
    shape = (CLIPS, FRAMES, H, W, C)
    position = jnp.arange(FRAMES).astype(jnp.float32) / float(max(FRAMES - 1, 1))
    flipped = jax.random.bernoulli(key_flip, 0.5, (CLIPS, 1))
    ramp = jnp.where(flipped, 1.0 - position[None, :], position[None, :])
    jitter = jax.random.uniform(key_frames, (CLIPS, FRAMES), jnp.float32, 0.0, math.log(10.0))
    frame_scale = jnp.exp(ramp * math.log(3.0) + jitter)
    chan_scale = jnp.exp(jax.random.uniform(key_chan, (C,), jnp.float32, 0.0, math.log(10.0)))
    base = jnp.clip(jax.random.normal(key_base, shape, jnp.float32), -6.0, 6.0)
    values = base * frame_scale[:, :, None, None, None] * chan_scale
    return values.astype(jnp.bfloat16)


def strengthened(values, stream_key, source, target, blocks, factor):
    owner, partner = [(jnp.arange(values.shape[dim]) // (values.shape[dim] // blocks)).reshape([-1 if axis == dim else 1 for axis in range(values.ndim)]) for dim in (source, target)]
    chosen = jax.random.permutation(stream_key, blocks)[partner]
    strong = (owner == chosen) | (owner == (partner + blocks // 2) % blocks)
    return jnp.where(strong, factor * values, values)


def block_levels(stream_key, shape, shards, low, top_value):
    loudness, own = 1.0, jax.random.fold_in(stream_key, 6)
    for dim, shards_of in shards:
        steps = jnp.exp(jax.random.uniform(jax.random.fold_in(own, dim), (shards_of,), jnp.float32, low / len(shards), top_value / len(shards)))
        loudness = loudness * jnp.repeat(steps, shape[dim] // shards_of).reshape([-1 if axis == dim else 1 for axis in range(len(shape))])
    return loudness


def scatter_about(rng, dims, spread, bound, cuts=(), dtype=jnp.bfloat16):
    entries = jax.random.normal(rng, dims, jnp.float32) * spread
    if len(cuts) > 0:
        entries = block_levels(rng, dims, cuts, -0.22, 0.18) * entries
    return jnp.clip(entries, min=-bound, max=bound).astype(dtype)


def heavy_noise(rng, extent, scale, most, pieces, heavy, kind=jnp.bfloat16):
    values = scale * jax.random.normal(rng, extent, jnp.float32)
    if pieces:
        values = values * block_levels(rng, extent, pieces, -0.22, 0.18)
    return jnp.clip(strengthened(values, jax.random.fold_in(rng, 3), *heavy), -most, most).astype(kind)


def setup_inputs(seed: int = 0) -> dict:
    keys = jax.random.split(jax.random.key(seed), 7)
    return {
        "activations": draw_activations(jax.random.fold_in(keys[6], 71), 0),
        "conv_weight": scatter_about(keys[1], (3, 3, 3, C, C), (27 * C) ** -0.5, 0.109375),
        "norm_gain": jnp.clip(jax.random.uniform(keys[2], (C,), jnp.float32, 0.5, 1.5), 0.5, 1.5),
        "norm_bias": jnp.clip(jax.random.uniform(keys[3], (C,), jnp.float32, -0.5, 0.5), -0.5, 0.5),
        "down_weight": scatter_about(keys[4], (3, 3, C, C2), (9 * C) ** -0.5, 0.1875),
        "cotangent": heavy_noise(keys[5], (CLIPS, FRAMES, H2, W2, C2), ((CLIPS * FRAMES * H2 * W2) ** -0.5 * 4), 0.625, ((0, 4), (2, 8)), (2, 4, 8, 2.0)),
    }


def clip_pass(inputs, grad_out, conv_weight, norm_gain, norm_bias, down_weight):
    inputs_f32 = inputs.astype(jnp.float32)[None]
    conv_out = lax.conv_general_dilated(inputs_f32, conv_weight.astype(jnp.float32), (1, 1, 1), [(2, 0), (1, 1), (1, 1)], dimension_numbers=('NDHWC', 'DHWIO', 'NDHWC'), precision=lax.Precision.HIGHEST)[0]
    grouped = conv_out.reshape(FRAMES, H, W, G, C // G)
    members = float(FRAMES * H * W * (C // G))
    group_sums = lax.optimization_barrier(jnp.sum(grouped, axis=(0, 1, 2, 4)))
    group_squares = lax.optimization_barrier(jnp.sum(grouped * grouped, axis=(0, 1, 2, 4)))
    group_mean = group_sums / members
    variance = group_squares / members - group_mean * group_mean
    inverse = lax.rsqrt(variance + 1e-06)
    normed = ((grouped - group_mean[:, None]) * inverse[:, None]).reshape(FRAMES, H, W, C) * norm_gain + norm_bias
    hidden = jax.nn.silu(normed).astype(jnp.bfloat16)
    hidden_f32 = hidden.astype(jnp.float32)

    def down_conv(weights):
        return lax.conv_general_dilated(hidden_f32, weights, (2, 2), [(0, 1), (0, 1)], dimension_numbers=('NHWC', 'HWIO', 'NHWC'), precision=lax.Precision.HIGHEST)
    encoded_clip, pullback = jax.vjp(down_conv, down_weight.astype(jnp.float32))
    grad_clip, = pullback(grad_out.astype(jnp.float32))
    return (encoded_clip.astype(jnp.bfloat16), grad_clip)

def reference(activations, conv_weight, norm_gain, norm_bias, down_weight, cotangent):

    def one_clip(pair):
        return clip_pass(pair[0], pair[1], conv_weight, norm_gain, norm_bias, down_weight)
    encoded, grads = lax.map(one_clip, (activations, cotangent))
    return (encoded, lax.optimization_barrier(jnp.sum(grads, axis=0)))
```

```python
import functools

import jax
import jax.numpy as jnp
from jax import lax
from jax.experimental import pallas as pl
from jax.experimental.pallas import tpu as pltpu
from jax.sharding import PartitionSpec as P

G = 32
VMEM = pl.BlockSpec(memory_space=pltpu.VMEM)
ANY = pl.BlockSpec(memory_space=pl.ANY)
F32 = jnp.float32
BF16 = jnp.bfloat16


def passed_along(shard, axis, by):
    count = lax.axis_size(axis)
    pairs = [(i, i + by) for i in range(count) if 0 <= i + by < count]
    return lax.ppermute(shard, axis, pairs)


def exchanged(shard, axis, bits):
    count = lax.axis_size(axis)
    return lax.ppermute(shard, axis, [(i, i ^ bits) for i in range(count)])


def gather_taps(x_ref, lhs):
    _, height, width, chans = x_ref.shape
    zero = jnp.zeros((1, width, chans), x_ref.dtype)
    for f in range(2):
        frame = x_ref[f]
        views = (
            jnp.concatenate([zero, frame[: height - 1]], axis=0),
            frame,
            jnp.concatenate([frame[1:], zero], axis=0),
        )
        for p in range(3):
            col = (3 * f + p) * chans
            lhs[:, col : col + chans] = views[p].reshape(height * width, chans)


def shifted_sum(wide, width):
    rows, lanes = wide.shape
    lanes = lanes // 3
    col = lax.broadcasted_iota(jnp.int32, (rows, lanes), 0) % width
    left = jnp.where(col == 0, 0.0, pltpu.roll(wide[:, :lanes], 1, 0))
    right = jnp.where(col == width - 1, 0.0, pltpu.roll(wide[:, 2 * lanes :], rows - 1, 0))
    return left + wide[:, lanes : 2 * lanes] + right


def own_kernel(x_ref, w_hbm, part_ref, early_ref, lhs, late, sems):
    _, height, width, chans = x_ref.shape
    copies = []
    for f in range(4):
        target = late if f >= 2 else early_ref
        for t in range(2):
            tap = f - t
            for q in range(3):
                cols = pl.ds((2 * q + t) * chans, chans)
                if 0 <= tap <= 2:
                    copy = pltpu.make_async_copy(
                        w_hbm.at[tap, :, q], target.at[f % 2, :, :, cols], sems.at[len(copies)]
                    )
                    copy.start()
                    copies.append(copy)
                else:
                    target[f % 2, :, :, cols] = jnp.zeros((3, chans, chans), BF16)
    gather_taps(x_ref, lhs)
    for copy in copies:
        copy.wait()
    weights = late[...].reshape(6 * chans, 6 * chans)
    block = 256
    for r in range(0, height * width, block):
        wide = jnp.dot(lhs[r : r + block], weights, preferred_element_type=F32)
        both = shifted_sum(wide, width)
        for t in range(2):
            part_ref[t, r : r + block] = both[:, t * chans : (t + 1) * chans]


def conv_kernel(x_ref, w_ref, part_ref, conv_ref, stats_ref, lhs):
    _, height, width, chans = x_ref.shape
    gather_taps(x_ref, lhs)
    weights = w_ref[...].reshape(6 * chans, 6 * chans)
    block = 256
    total = jnp.zeros((1, chans), F32)
    squares = jnp.zeros((1, chans), F32)
    for r in range(0, height * width, block):
        wide = jnp.dot(lhs[r : r + block], weights, preferred_element_type=F32)
        both = shifted_sum(wide, width)
        for t in range(2):
            value = both[:, t * chans : (t + 1) * chans] + part_ref[t, r : r + block]
            conv_ref[t, r : r + block] = value
            total = total + jnp.sum(value, axis=0, keepdims=True)
            squares = squares + jnp.sum(value * value, axis=0, keepdims=True)
    tile = jnp.concatenate([total, squares, jnp.zeros((6, chans), F32)], axis=0)
    for k in range(stats_ref.shape[0]):
        stats_ref[k] = tile


def group_sum(tile, size):
    lanes = tile.shape[-1]
    lane = lax.broadcasted_iota(jnp.int32, tile.shape, 1)
    step = 1
    while step < size:
        up = pltpu.roll(tile, lanes - step, 1)
        down = pltpu.roll(tile, step, 1)
        tile = tile + jnp.where((lane // step) % 2 == 0, up, down)
        step *= 2
    return tile


def down_kernel(members, width, conv_ref, stats_ref, affine_ref, w_ref, cot_ref, enc_ref, grad_ref, patch):
    frames, cells, chans = conv_ref.shape
    rows = cells // width
    half = width // 2
    sums = stats_ref[0]
    for k in range(1, stats_ref.shape[0]):
        sums = sums + stats_ref[k]
    sums = group_sum(sums, chans // G) / members
    mean = sums[0:1]
    variance = sums[1:2] - mean * mean
    scale = lax.rsqrt(variance + 1e-06) * affine_ref[0:1] * 0.5
    shift = affine_ref[1:2] * 0.5

    def silu(value):
        u = (value - mean) * scale + shift
        return u + u * jnp.tanh(u)

    outs = rows // 2 * half
    for t in range(frames):
        even = silu(conv_ref[t, pl.ds(0, rows * half, stride=2)])
        odd = silu(conv_ref[t, pl.ds(1, rows * half, stride=2)])
        col = lax.broadcasted_iota(jnp.int32, even.shape, 0) % half
        after = jnp.where(col == half - 1, 0.0, pltpu.roll(even, rows * half - 1, 0))
        for q, cells_q in enumerate((even, odd, after)):
            split = cells_q.reshape(rows // 2, 2, half, chans)
            below = jnp.concatenate([split[1:, 0], jnp.zeros((1, half, chans), F32)], axis=0)
            for p, view in enumerate((split[:, 0], split[:, 1], below)):
                tap = (3 * p + q) * chans
                patch[t * outs : (t + 1) * outs, tap : tap + chans] = view.reshape(outs, chans).astype(BF16)
    values = patch[...]
    enc_ref[...] = jnp.dot(values, w_ref[...], preferred_element_type=F32).astype(BF16)
    grad = lax.dot_general(cot_ref[...], values, (((0,), (0,)), ((), ())), preferred_element_type=F32)
    for tap in range(9):
        grad_ref[tap] = grad[:, tap * chans : (tap + 1) * chans].astype(BF16)


def pick(array, index, axis):
    return lax.dynamic_index_in_dim(array, index, axis, keepdims=False)


def joined(mine, other, bit, axis):
    low = jnp.where(bit == 0, mine, other)
    high = jnp.where(bit == 0, other, mine)
    return jnp.stack([low, high], axis=axis)


def per_device(activations, conv_weight, norm_gain, norm_bias, down_weight, cotangent):
    _, frames, height, width, chans = activations.shape
    n = lax.axis_size("tm")
    bits = n.bit_length() - 1
    me = lax.axis_index("tm")
    bit = [(me >> s) & 1 for s in range(bits)]
    cells = height * width
    half_cells = (height // 2) * (width // 2)
    params = pltpu.CompilerParams(vmem_limit_bytes=32 * 1024 * 1024)
    own = activations[0]

    earlier = passed_along(own, "tm", 1)

    rows_dev = (height // 2) // n
    cot = cotangent.reshape((2,) * bits + (frames, rows_dev * (width // 2), chans))
    for s in range(bits):
        axis = bits - 1 - s
        other = exchanged(pick(cot, 1 - bit[s], axis), "tm", 1 << s)
        cot = joined(pick(cot, bit[s], axis), other, bit[s], axis + 1)
    cot = cot.reshape(frames * half_cells, chans)

    part, early = pl.pallas_call(
        own_kernel,
        out_shape=(
            jax.ShapeDtypeStruct((frames, cells, chans), F32),
            jax.ShapeDtypeStruct((2, 3, chans, 6 * chans), BF16),
        ),
        in_specs=[VMEM, ANY],
        out_specs=(VMEM, VMEM),
        scratch_shapes=[
            pltpu.VMEM((cells, 6 * chans), BF16),
            pltpu.VMEM((2, 3, chans, 6 * chans), BF16),
            pltpu.SemaphoreType.DMA((18,)),
        ],
        compiler_params=params,
        cost_estimate=pl.CostEstimate(flops=2 * cells * 36 * chans * chans, bytes_accessed=2**21, transcendentals=0),
        name="own_frames",
    )(own, conv_weight)

    conv, stats = pl.pallas_call(
        conv_kernel,
        out_shape=(
            jax.ShapeDtypeStruct((frames, cells, chans), F32),
            jax.ShapeDtypeStruct((n, 8, chans), F32),
        ),
        in_specs=[VMEM, VMEM, VMEM],
        out_specs=(VMEM, VMEM),
        scratch_shapes=[pltpu.VMEM((cells, 6 * chans), BF16)],
        compiler_params=params,
        cost_estimate=pl.CostEstimate(flops=2 * cells * 36 * chans * chans, bytes_accessed=2**21, transcendentals=0),
        name="earlier_frames",
    )(earlier, early, part)

    stats = lax.all_to_all(stats, "tm", split_axis=0, concat_axis=0, tiled=True)
    affine = jnp.stack([norm_gain, norm_bias])
    members = float(frames * n * cells * (chans // G))

    enc, grad = pl.pallas_call(
        functools.partial(down_kernel, members, width),
        out_shape=(
            jax.ShapeDtypeStruct((frames * half_cells, chans), BF16),
            jax.ShapeDtypeStruct((9, chans, chans), BF16),
        ),
        in_specs=[VMEM] * 5,
        out_specs=(VMEM, VMEM),
        scratch_shapes=[pltpu.VMEM((frames * half_cells, 9 * chans), BF16)],
        compiler_params=params,
        name="down",
    )(conv, stats, affine, down_weight.reshape(9 * chans, chans), cot)

    share = chans // n
    grad = grad.reshape((9,) + (2,) * bits + (share, chans))
    enc = enc.reshape((frames,) + (2,) * bits + (rows_dev * (width // 2), chans))
    for s in range(bits):
        axis = bits - s
        keep_g, send_g = pick(grad, bit[s], axis), pick(grad, 1 - bit[s], axis)
        keep_e, send_e = pick(enc, bit[s], axis), pick(enc, 1 - bit[s], axis)
        packed = jnp.concatenate([send_g.reshape(-1, chans), send_e.reshape(-1, chans)], axis=0)
        packed = exchanged(packed, "tm", 1 << s)
        cut = send_g.size // chans
        grad = (keep_g.astype(F32) + packed[:cut].reshape(keep_g.shape).astype(F32)).astype(BF16)
        enc = joined(keep_e, packed[cut:].reshape(keep_e.shape), bit[s], 0)
        enc = enc.reshape((-1,) + keep_e.shape[1:])
    encoded = enc.reshape(1, frames * n, rows_dev, width // 2, chans)

    dp = lax.axis_size("dp")
    terms = [grad.astype(F32)] + [exchanged(grad, "dp", b).astype(F32) for b in range(1, dp)]
    while len(terms) > 1:
        terms = [terms[i] + terms[i + 1] for i in range(0, len(terms), 2)]
    grad_down = jnp.swapaxes(terms[0], 1, 2).reshape(3, 3, chans, share)
    return encoded, grad_down


def solution(mesh):
    placed = (P("dp", "tm", None, None, None), P(), P(), P(), P(), P("dp", None, "tm", None, None))
    return jax.shard_map(
        per_device,
        mesh=mesh,
        in_specs=placed,
        out_specs=(P("dp", None, "tm", None, None), P(None, None, None, "tm")),
        check_vma=False,
    )
```
